128 devices in a mesh: dp: 4 (over z), fsdp: 32 (over x, y, core).
Axes of the slice: x: 4, y: 4, z: 4, core: 2. Of those that a mesh axis runs over, the one named last changes fastest.
Arguments:
- weight_up: bfloat16 [8192, 16384], P('dp', 'fsdp'), may hold values from -6 to 6
- weight_down: bfloat16 [16384, 8192], P('dp', 'fsdp'), may hold values from -6 to 6
- grad_up: bfloat16 [4, 8192, 16384], P('dp', None, 'fsdp'), may hold values from -6 to 6
- grad_down: bfloat16 [4, 16384, 8192], P('dp', None, 'fsdp'), may hold values from -8 to 8
- basis_up: bfloat16 [8192, 256], P('fsdp'), may hold values from -0.0625 to 0.0625
- basis_down: bfloat16 [8192, 256], P('fsdp'), may hold values from -0.0625 to 0.0625
- moment_up: float32 [256, 16384], P('dp', 'fsdp'), may hold values from -4 to 4
- second_up: float32 [256, 16384], P('dp', 'fsdp'), may hold values from 0.2 to 2
- moment_down: float32 [16384, 256], P(('dp', 'fsdp')), may hold values from -4 to 4
- second_down: float32 [16384, 256], P(('dp', 'fsdp')), may hold values from 0.2 to 2
Outputs:
- new_weight_up: bfloat16 [8192, 16384], P('dp', 'fsdp')
- new_weight_down: bfloat16 [16384, 8192], P('dp', 'fsdp')
- new_moment_up: float32 [256, 16384], P('dp', 'fsdp')
- new_second_up: float32 [256, 16384], P('dp', 'fsdp')
- new_moment_down: float32 [16384, 256], P(('dp', 'fsdp'))
- new_second_down: float32 [16384, 256], P(('dp', 'fsdp'))
The draws below stay inside these ranges and needn't reach their ends.
All inputs are finite; a program needn't handle non-finite values.
Results may differ from the reference program's by a relative error of at most 0.0055.
Values may be sent and summed in bfloat16 or wider, within the bound.
No kernel may reach another device: no remote copies, remote signals or barrier semaphores. Data moves between devices by JAX's collectives and lax.ppermute only.
A program may use at most 128 MiB of HBM per device.

```python
import math
import jax
import jax.numpy as jnp
from jax import lax

D = 8192
FF = 16384
RANK = 256
ADAM_STEP = 10
REPL = 4


def spiked(entries, key, source, target, shards_of, factor):
    owner, partner = [(jnp.arange(entries.shape[axis_at]) // (entries.shape[axis_at] // shards_of)).reshape([-1 if axis == axis_at else 1 for axis in range(entries.ndim)]) for axis_at in (source, target)]
    chosen = jax.random.permutation(key, shards_of)[partner]
    strong = (owner == chosen) | (owner == (partner + shards_of // 2) % shards_of)
    return jnp.where(strong, factor * entries, entries)


def block_levels(stream_key, dims, pieces, low, top_value):
    gain = 1.0
    for axis_at, shards_of in pieces:
        heights = jax.random.uniform(jax.random.fold_in(jax.random.fold_in(stream_key, 6), axis_at), (shards_of,), jnp.float32, low / len(pieces), top_value / len(pieces))
        gain = gain * jnp.repeat(jnp.exp(heights), dims[axis_at] // shards_of).reshape((-1,) + (1,) * (len(dims) - 1 - axis_at))
    return gain


def noise(stream_key, shape, scale, limit, shards=(), kind=jnp.bfloat16):
    values = jax.random.normal(stream_key, shape, jnp.float32) * scale
    if len(shards) > 0:
        values = block_levels(stream_key, shape, shards, -0.22, 0.18) * values
    return jnp.clip(values, min=-limit, max=limit).astype(kind)


def heavy_noise(rng, shape, deviation, bound, shards, heavy, dtype=jnp.bfloat16):
    drawn = deviation * jax.random.normal(rng, shape, jnp.float32)
    if shards:
        drawn = drawn * block_levels(rng, shape, shards, -0.22, 0.18)
    return jnp.clip(spiked(drawn, jax.random.fold_in(rng, 3), *heavy), -bound, bound).astype(dtype)


def setup_inputs(seed: int = 0) -> dict:
    splits = jax.random.split(jax.random.key(seed), 11)
    return {
        "weight_up": noise(splits[0], (D, FF), 1.0, 6.0, ((0, 4), (1, 32))),
        "weight_down": noise(splits[1], (FF, D), 1.0, 6.0, ((0, 4), (1, 32))),
        "grad_up": noise(splits[2], (REPL, D, FF), 1.0, 6.0, ((0, 4), (2, 32))),
        "grad_down": heavy_noise(splits[3], (REPL, FF, D), 1.0, 8.0, ((0, 4), (2, 32)), (2, 1, 32, 2.75)),
        "basis_up": noise(splits[4], (D, RANK), D ** -0.5, 0.0625, ((0, 32),)),
        "basis_down": noise(splits[5], (D, RANK), D ** -0.5, 0.0625, ((0, 32),)),
        "moment_up": noise(splits[6], (RANK, FF), 0.5, 4.0, ((0, 4), (1, 32)), jnp.float32),
        "second_up": jnp.clip(jnp.exp(math.log(2.0) - 2.3025851 * jax.random.uniform(splits[7], (RANK, FF), jnp.float32) ** block_levels(splits[7], (RANK, FF), ((0, 4), (1, 32)), -0.2, 0.2)), 0.2, 2.0),
        "moment_down": noise(splits[8], (FF, RANK), 0.5, 4.0, ((0, 128),), jnp.float32),
        "second_down": jnp.clip(jnp.exp(math.log(2.0) - 2.3025851 * jax.random.uniform(splits[9], (FF, RANK), jnp.float32) ** block_levels(splits[9], (FF, RANK), ((0, 128),), -0.2, 0.2)), 0.2, 2.0),
    }


first_decay = 0.9
second_decay = 0.99
adam_eps = 1e-08
norm_eps = 1e-06
learn_rate = 0.5

def adam_update(mean_grad, first, second):
    new_first = first_decay * first + (1.0 - first_decay) * mean_grad
    new_second = second_decay * second + (1.0 - second_decay) * mean_grad * mean_grad
    corr_first = 1.0 - first_decay ** ADAM_STEP
    corr_second = 1.0 - second_decay ** ADAM_STEP
    update = (new_first / corr_first / (jnp.sqrt(new_second / corr_second) + adam_eps)).astype(jnp.bfloat16)
    return (new_first, new_second, update)

def reference(weight_up, weight_down, grad_up, grad_down, basis_up, basis_down, moment_up, second_up, moment_down, second_down):
    proj_up = jnp.zeros((RANK, FF), jnp.float32)
    proj_down = jnp.zeros((FF, RANK), jnp.float32)
    for index in range(REPL):
        proj_up = proj_up + lax.dot_general(basis_up, grad_up[index], (((0,), (0,)), ((), ())), preferred_element_type=jnp.float32)
        proj_down = proj_down + jnp.dot(grad_down[index], basis_down, preferred_element_type=jnp.float32)
    proj_up = proj_up * (1.0 / REPL)
    proj_down = proj_down * (1.0 / REPL)
    new_moment_up, new_second_up, low_up = adam_update(proj_up, moment_up, second_up)
    new_moment_down, new_second_down, low_down = adam_update(proj_down, moment_down, second_down)
    delta_up = jnp.dot(basis_up, low_up, preferred_element_type=jnp.float32)
    delta_down = lax.dot_general(low_down, basis_down, (((1,), (1,)), ((), ())), preferred_element_type=jnp.float32)
    weight_upf = weight_up.astype(jnp.float32)
    weight_downf = weight_down.astype(jnp.float32)
    ratio_up = jnp.sqrt(jnp.sum(weight_upf * weight_upf)) / (jnp.sqrt(jnp.sum(delta_up * delta_up)) + norm_eps)
    ratio_down = jnp.sqrt(jnp.sum(weight_downf * weight_downf)) / (jnp.sqrt(jnp.sum(delta_down * delta_down)) + norm_eps)
    new_weight_up = (weight_upf - learn_rate * ratio_up * delta_up).astype(jnp.bfloat16)
    new_weight_down = (weight_downf - learn_rate * ratio_down * delta_down).astype(jnp.bfloat16)
    return (new_weight_up, new_weight_down, new_moment_up, new_second_up, new_moment_down, new_second_down)
```

```python
import functools

import jax
import jax.numpy as jnp
from jax import lax
from jax.experimental import pallas as pl
from jax.experimental.pallas import tpu as pltpu
from jax.sharding import Mesh, PartitionSpec as P

ADAM_STEP = 10

first_decay = 0.9
second_decay = 0.99
adam_eps = 1e-08
norm_eps = 1e-06
learn_rate = 0.5

f32 = jnp.float32
bf16 = jnp.bfloat16

AXES = ("z", "x", "y", "c")
SIZES = (4, 4, 4, 2)


def adam_update(mean_grad, first, second):
    new_first = first_decay * first + (1.0 - first_decay) * mean_grad
    new_second = second_decay * second + (1.0 - second_decay) * mean_grad * mean_grad
    corr_first = 1.0 - first_decay**ADAM_STEP
    corr_second = 1.0 - second_decay**ADAM_STEP
    update = (new_first / corr_first / (jnp.sqrt(new_second / corr_second) + adam_eps)).astype(
        bf16
    )
    return (new_first, new_second, update)


def shift_pairs(axis0, axis1, k):
    pairs = []
    for source in range(128):
        coords = [source // 32, source // 8 % 4, source // 2 % 4, source % 2]
        dim = AXES.index(axis1 if coords[3] else axis0)
        coords[dim] = (coords[dim] + k) % 4
        target = ((coords[0] * 4 + coords[1]) * 4 + coords[2]) * 2 + coords[3]
        pairs.append((source, target))
    return pairs


def shift(value, axis0, axis1, k):
    return lax.ppermute(value, AXES, shift_pairs(axis0, axis1, k))


def swap_cores(value):
    return lax.ppermute(value, "c", [(0, 1), (1, 0)])


def pick(stacked, index):
    return lax.dynamic_index_in_dim(stacked, index, 0, keepdims=False)


def place_of(place, own):
    return place[2] if own else 1 - place[2]


def project_kernel(has_other, place_ref, *refs):
    grad_refs, basis_ref, out_ref = refs[:4], refs[4], refs[-1]
    for part, grad_ref in enumerate(grad_refs):
        rows = grad_ref[...].reshape(512, 256)
        out = jnp.dot(rows, basis_ref[...], preferred_element_type=f32)
        if has_other:
            out = out + refs[5][0, part].reshape(512, 256).astype(f32)
        out_ref[0, part] = out.astype(bf16).reshape(4, 128, 256)


def project_rows(place, grad, basis, own, shifts, other=None, other_at=0):
    def grad_map(part):
        def index(step, place):
            core = place_of(place, own)
            ahead = shifts[-1]
            for i, shift_by in enumerate(shifts[:-1]):
                ahead = jnp.where(step == i, shift_by, ahead)
            block = (jnp.where(core == 0, place[0], place[1]) + ahead) % 4
            return (
                jnp.where(core == 0, block, part),
                jnp.where(core == 0, part, block),
                0,
                core,
                0,
                0,
            )

        return index

    tile = (1, 4, 4, 128, 256)
    in_specs = [pl.BlockSpec((1, 1, 4, 1, 128, 256), grad_map(part)) for part in range(4)]
    in_specs.append(pl.BlockSpec((256, 256), lambda step, place: (0, 0)))
    operands = [place, grad, grad, grad, grad, basis]
    if other is not None:
        in_specs.append(pl.BlockSpec(tile, lambda step, place: (other_at, 0, 0, 0, 0)))
        operands.append(other)
    count = len(shifts)
    return pl.pallas_call(
        functools.partial(project_kernel, other is not None),
        out_shape=jax.ShapeDtypeStruct((count, 4, 4, 128, 256), bf16),
        grid_spec=pltpu.PrefetchScalarGridSpec(
            num_scalar_prefetch=1,
            grid=(count,),
            in_specs=in_specs,
            out_specs=pl.BlockSpec(tile, lambda step, place: (step, 0, 0, 0, 0)),
        ),
        compiler_params=pltpu.CompilerParams(vmem_limit_bytes=24 << 20),
        cost_estimate=pl.CostEstimate(
            flops=count, bytes_accessed=count, transcendentals=0
        ),
    )(*operands)


def project_up_kernel(place_ref, basis_ref, *refs):
    grad_refs, before_ref, out_ref, sum_ref = refs[:8], refs[8:-2], refs[-2], refs[-1]
    step = pl.program_id(0)

    @pl.when(step == 0)
    def _():
        sum_ref[...] = before_ref[0][...] if before_ref else jnp.zeros_like(sum_ref)

    parts = [
        lax.dot_general(
            basis_ref[part // 4, part % 4],
            grad_ref[...],
            (((0,), (0,)), ((), ())),
            preferred_element_type=f32,
        )
        for part, grad_ref in enumerate(grad_refs)
    ]
    sum_ref[...] += functools.reduce(lambda a, b: a + b, parts)

    @pl.when(step == 1)
    def _():
        out_ref[...] = sum_ref[...].astype(out_ref.dtype)


def project_up(place, basis, grad, own, before=None):
    def grad_map(part):
        def index(step, place):
            x = (place[1] + 4 - part % 4) % 4
            y = (place[3] + 4 - part // 4 - 2 * step) % 4
            return ((x * 4 + y) * 2 + place_of(place, own), 0)

        return index

    whole = pl.BlockSpec((256, 512), lambda step, place: (0, 0))
    in_specs = [pl.BlockSpec((2, 4, 256, 256), lambda step, place: (step, 0, 0, 0))]
    in_specs += [pl.BlockSpec((256, 512), grad_map(part)) for part in range(8)]
    operands = [place, basis] + [grad] * 8
    if before is not None:
        in_specs.append(whole)
        operands.append(before)
    return pl.pallas_call(
        project_up_kernel,
        out_shape=jax.ShapeDtypeStruct((256, 512), f32 if before is None else bf16),
        grid_spec=pltpu.PrefetchScalarGridSpec(
            num_scalar_prefetch=1,
            grid=(2,),
            in_specs=in_specs,
            out_specs=whole,
            scratch_shapes=[pltpu.VMEM((256, 512), f32)],
        ),
        compiler_params=pltpu.CompilerParams(vmem_limit_bytes=60 << 20),
        cost_estimate=pl.CostEstimate(
            flops=1, bytes_accessed=1, transcendentals=0
        ),
    )(*operands)


def sum_kernel(place_ref, own_ref, *refs):
    got_refs, next_ref, out_refs = refs[:3], refs[3], refs[4:]
    start = jnp.where(place_ref[2] == 0, place_ref[1], place_ref[0])
    for ahead, out_ref in zip((0, 2, 1, 3), (next_ref, *out_refs), strict=True):
        at = (start + ahead) % 4
        value = own_ref[at].astype(f32)
        for got_ref in got_refs:
            value = value + got_ref[at].astype(f32)
        out_ref[...] = value.astype(out_ref.dtype)


def sum_blocks(place, own, got):
    vmem = pl.BlockSpec(memory_space=pltpu.VMEM)
    block = jax.ShapeDtypeStruct((4, 128, 256), bf16)
    return pl.pallas_call(
        sum_kernel,
        out_shape=[jax.ShapeDtypeStruct((4, 128, 256), f32), block, block, block],
        in_specs=[pl.BlockSpec(memory_space=pltpu.SMEM)] + [vmem] * 4,
        out_specs=[vmem] * 4,
        compiler_params=pltpu.CompilerParams(vmem_limit_bytes=24 << 20),
        cost_estimate=pl.CostEstimate(flops=4 << 20, bytes_accessed=5 << 20, transcendentals=0),
    )(place, own, *got)


def norms_kernel(weights_ref, *refs):
    low_refs, (basis_down_ref, other_down_ref) = refs[:4], refs[4:6]
    own_ref, other_ref, low_up_ref, out_ref = refs[6:]

    def square_sum(delta):
        return jnp.sum(jnp.sum(delta * delta, axis=0, keepdims=True), axis=1, keepdims=True)

    up = jnp.zeros((1, 1), f32)
    for ref in (own_ref, other_ref):
        for block in range(4):
            up += square_sum(jnp.dot(ref[block], low_up_ref[...], preferred_element_type=f32))
    down = jnp.zeros((1, 1), f32)
    for low_ref in low_refs:
        for ref in (basis_down_ref, other_down_ref):
            down += square_sum(
                lax.dot_general(
                    low_ref[...].reshape(512, 256),
                    ref[...],
                    (((1,), (1,)), ((), ())),
                    preferred_element_type=f32,
                )
            )
    lane = lax.broadcasted_iota(jnp.int32, (1, 128), 1)
    row = jnp.where(lane == 0, weights_ref[0], weights_ref[1])
    row = jnp.where(lane == 2, up, jnp.where(lane == 3, down, row))
    out_ref[...] = jnp.broadcast_to(row[None], out_ref.shape)


def norms(weight_sums, lows, basis_down, other_down, own, other, low_up):
    vmem = pl.BlockSpec(memory_space=pltpu.VMEM)
    operands = [weight_sums, *lows, basis_down, other_down, own, other, low_up]
    return pl.pallas_call(
        norms_kernel,
        out_shape=jax.ShapeDtypeStruct((128, 1, 128), f32),
        in_specs=[pl.BlockSpec(memory_space=pltpu.SMEM)] + [vmem] * (len(operands) - 1),
        out_specs=vmem,
        compiler_params=pltpu.CompilerParams(vmem_limit_bytes=16 << 20),
        cost_estimate=pl.CostEstimate(
            flops=1 << 34, bytes_accessed=3 << 20, transcendentals=0
        ),
    )(*operands)


def update_kernel(place_ref, sums_ref, *refs):
    low_refs, (basis_down_ref, weight_down_ref) = refs[:8], refs[8:10]
    own_ref, other_ref, low_up_ref, weight_up_ref, up_ref, down_ref = refs[10:]
    sums = jnp.sum(sums_ref[...], axis=0)
    scale_up = learn_rate * (jnp.sqrt(sums[:, 0:1]) / (jnp.sqrt(sums[:, 2:3]) + norm_eps))
    scale_down = learn_rate * (jnp.sqrt(sums[:, 1:2]) / (jnp.sqrt(sums[:, 3:4]) + norm_eps))
    core0 = place_ref[2]
    for back in range(4):
        y = (place_ref[3] + 4 - back) % 4
        for basis_ref, core in ((own_ref, core0), (other_ref, 1 - core0)):
            delta = jnp.dot(basis_ref[back], low_up_ref[...], preferred_element_type=f32)
            old = weight_up_ref[y, core].astype(f32)
            up_ref[y, core] = (old - scale_up * delta).astype(bf16)
    for i, low_ref in enumerate(low_refs):
        outer = i % 4
        core = core0 if i < 4 else 1 - core0
        delta = lax.dot_general(
            low_ref[...].reshape(512, 256),
            basis_down_ref[...],
            (((1,), (1,)), ((), ())),
            preferred_element_type=f32,
        )
        for inner in range(4):
            x = (place_ref[1] + 4 - jnp.where(core == 0, outer, inner)) % 4
            y = (place_ref[3] + 4 - jnp.where(core == 0, inner, outer)) % 4
            old = weight_down_ref[x, y, core].astype(f32)
            down_ref[x, y, core] = (
                old - scale_down * delta[inner * 128 : (inner + 1) * 128]
            ).astype(bf16)


def update(place, sums, lows, basis_down, weight_down, own, other, low_up, weight_up):
    vmem = pl.BlockSpec(memory_space=pltpu.VMEM)
    operands = [place, sums, *lows, basis_down, weight_down, own, other, low_up, weight_up]
    return pl.pallas_call(
        update_kernel,
        out_shape=[
            jax.ShapeDtypeStruct(weight_up.shape, bf16),
            jax.ShapeDtypeStruct(weight_down.shape, bf16),
        ],
        in_specs=[pl.BlockSpec(memory_space=pltpu.SMEM)] + [vmem] * (len(operands) - 1),
        out_specs=[vmem, vmem],
        compiler_params=pltpu.CompilerParams(vmem_limit_bytes=16 << 20),
        cost_estimate=pl.CostEstimate(
            flops=4 * 2048 * 256 * 512, bytes_accessed=11 << 20, transcendentals=0
        ),
    )(*operands)


def after(value, *others):
    return lax.optimization_barrier((value, *others))[0]


def total(stages, first):
    return functools.reduce(lambda a, b: a + b.astype(f32), stages, first.astype(f32))


def per_device(
    weight_up,
    weight_down,
    grad_up,
    grad_down,
    basis_up,
    basis_down,
    moment_up,
    second_up,
    moment_down,
    second_down,
):
    z, x, y, c = (lax.axis_index(a) for a in AXES)
    replicas = 4
    local_up = grad_up[0]
    local_down = grad_down[0].reshape(4, 4, 4, 2, 128, 256)

    place = jnp.stack([z, x, c, y]).astype(jnp.int32)

    near = jnp.stack([basis_up] + [shift(basis_up, "x", "x", k) for k in (1, 2, 3)])
    weight_upf = weight_up.astype(f32)
    weight_downf = weight_down.astype(f32)
    wsq_up = jnp.sum(weight_upf * weight_upf)
    wsq_down = jnp.sum(weight_downf * weight_downf)

    other_basis_down = swap_cores(basis_down)
    place = after(place, other_basis_down)
    half = functools.partial(project_rows, place, local_down, basis_down, False)
    whole = functools.partial(project_rows, place, local_down, basis_down, True)
    half_2 = half((2,))
    got_2 = swap_cores(half_2)
    ready = {2: whole((2,), got_2)[0]}
    half_130 = project_rows(
        after(place, half_2, near), local_down, basis_down, False, (1, 3, 0)
    )
    got_130 = swap_cores(half_130)
    ready[1] = whole((1,), got_130, 0)[0]
    ready[3] = whole((3,), after(got_130, ready[1]), 1)[0]
    ready[0] = whole((0,), after(got_130, ready[3]), 2)[0]
    one = [shift(ready[k], "z", "x", k) for k in (2, 1, 3)]

    two_own, *two = sum_blocks(after(place, wsq_up, wsq_down), ready[0], one)
    two = [two_own] + [shift(t, "x", "z", k) for t, k in zip(two, (2, 1, 3))]

    back, ahead = shift(near, "y", "y", 1), shift(near, "y", "y", 3)
    back_half, ahead_half = after(back[:2], two[0]), after(ahead[2:], two[0])
    far = jnp.concatenate([shift(back_half, "y", "y", 1), shift(ahead_half, "y", "y", 3)])
    own_basis = jnp.stack([near, back, far, ahead])
    own_basis = after(own_basis, *two[1:])
    other_basis = swap_cores(own_basis)

    partial_up = project_up(place, own_basis, local_up, True)
    two[0] = after(two[0], partial_up)
    partial_up = project_up(place, other_basis, local_up, False, partial_up)
    partial_up = partial_up.reshape(4, 64, 512)

    def part_three(k):
        index = (y + k) % 4
        return total([pick(t, index) for t in two[1:]], pick(two[0], index))

    three = [part_three(0)] + [
        shift(part_three(k).astype(bf16), "y", "y", k) for k in (2, 1, 3)
    ]
    three[0] = after(three[0], partial_up)
    proj_down = total(three[1:], three[0]) * (1.0 / replicas)
    new_moment_down, new_second_down, low_down = adam_update(proj_down, moment_down, second_down)

    up = [pick(partial_up, z)] + [
        shift(pick(partial_up, (z + k) % 4), "z", "z", k) for k in (2, 1, 3)
    ]
    proj_up = total(up[1:], up[0]) * (1.0 / replicas)
    new_moment_up, new_second_up, low_up = adam_update(proj_up, moment_up, second_up)
    gathered = jnp.stack([low_up] + [shift(low_up, "z", "z", k) for k in (1, 2, 3)])
    gathered = jnp.stack([pick(gathered, (z + 4 - block) % 4) for block in range(4)])
    all_low_up = gathered.reshape(256, 512)

    blocks = [
        lax.dynamic_index_in_dim(basis, (x + 4 - z) % 4, 1, keepdims=False)
        for basis in (own_basis, other_basis)
    ]

    inner = jnp.stack([low_down] + [shift(low_down, "y", "x", k) for k in (1, 2, 3)])
    outer = [inner] + [shift(inner, "x", "y", k) for k in (1, 2, 3)]
    sibling = [swap_cores(low) for low in outer]

    sums = norms(
        jnp.stack([wsq_up, wsq_down]),
        outer,
        basis_down,
        other_basis_down,
        *blocks,
        all_low_up,
    )
    sums = lax.all_to_all(sums, AXES, 0, 0, tiled=True)
    new_weight_up, new_weight_down = update(
        place,
        sums,
        outer + sibling,
        basis_down,
        weight_down.reshape(4, 4, 2, 128, 256),
        *blocks,
        all_low_up,
        weight_up.reshape(4, 2, 256, 512),
    )
    new_weight_up = new_weight_up.reshape(2048, 512)
    new_weight_down = new_weight_down.reshape(4096, 256)
    return (
        new_weight_up,
        new_weight_down,
        new_moment_up,
        new_second_up,
        new_moment_down,
        new_second_down,
    )


def solution(mesh):
    devices = Mesh(mesh.devices.reshape(SIZES), AXES)
    columns = ("x", "y", "c")
    in_specs = (
        P("z", columns),
        P("z", columns),
        P("z", None, columns),
        P("z", None, columns),
        P(columns, None),
        P(columns, None),
        P("z", columns),
        P("z", columns),
        P(AXES, None),
        P(AXES, None),
    )
    out_specs = (
        P("z", columns),
        P("z", columns),
        P("z", columns),
        P("z", columns),
        P(AXES, None),
        P(AXES, None),
    )
    return jax.shard_map(
        per_device, mesh=devices, in_specs=in_specs, out_specs=out_specs, check_vma=False
    )
```

```python
import functools

import jax
import jax.numpy as jnp
from jax import lax
from jax.experimental import pallas as pl
from jax.experimental.pallas import tpu as pltpu
from jax.sharding import Mesh, PartitionSpec as P

ADAM_STEP = 10

first_decay = 0.9
second_decay = 0.99
adam_eps = 1e-08
norm_eps = 1e-06
learn_rate = 0.5

f32 = jnp.float32
bf16 = jnp.bfloat16

AXES = ("z", "x", "y", "c")
SIZES = (4, 4, 4, 2)


def adam_update(mean_grad, first, second):
    new_first = first_decay * first + (1.0 - first_decay) * mean_grad
    new_second = second_decay * second + (1.0 - second_decay) * mean_grad * mean_grad
    corr_first = 1.0 - first_decay**ADAM_STEP
    corr_second = 1.0 - second_decay**ADAM_STEP
    update = (new_first / corr_first / (jnp.sqrt(new_second / corr_second) + adam_eps)).astype(
        bf16
    )
    return (new_first, new_second, update)


def shift_pairs(axis0, axis1, k):
    pairs = []
    for source in range(128):
        coords = [source // 32, source // 8 % 4, source // 2 % 4, source % 2]
        dim = AXES.index(axis1 if coords[3] else axis0)
        coords[dim] = (coords[dim] + k) % 4
        target = ((coords[0] * 4 + coords[1]) * 4 + coords[2]) * 2 + coords[3]
        pairs.append((source, target))
    return pairs


def shift(value, axis0, axis1, k):
    return lax.ppermute(value, AXES, shift_pairs(axis0, axis1, k))


def swap_cores(value):
    return lax.ppermute(value, "c", [(0, 1), (1, 0)])


def exchange(value, mask):
    return lax.ppermute(value, "z", [(i, i ^ mask) for i in range(4)])


def pick(stacked, index):
    return lax.dynamic_index_in_dim(stacked, index, 0, keepdims=False)


def place_of(place, own):
    return place[2] if own else 1 - place[2]


def project_kernel(has_other, place_ref, *refs):
    grad_refs, basis_ref, out_ref = refs[:4], refs[4], refs[-1]
    for part, grad_ref in enumerate(grad_refs):
        rows = grad_ref[...].reshape(512, 256)
        out = jnp.dot(rows, basis_ref[...], preferred_element_type=f32)
        if has_other:
            out = out + refs[5][0, part].reshape(512, 256).astype(f32)
        out_ref[0, part] = out.astype(bf16).reshape(4, 128, 256)


def project_rows(place, grad, basis, own, shifts, other=None, other_at=0):
    def grad_map(part):
        def index(step, place):
            core = place_of(place, own)
            ahead = shifts[-1]
            for i, shift_by in enumerate(shifts[:-1]):
                ahead = jnp.where(step == i, shift_by, ahead)
            block = (jnp.where(core == 0, place[0], place[1]) + ahead) % 4
            return (
                jnp.where(core == 0, block, part),
                jnp.where(core == 0, part, block),
                0,
                core,
                0,
                0,
            )

        return index

    tile = (1, 4, 4, 128, 256)
    in_specs = [pl.BlockSpec((1, 1, 4, 1, 128, 256), grad_map(part)) for part in range(4)]
    in_specs.append(pl.BlockSpec((256, 256), lambda step, place: (0, 0)))
    operands = [place, grad, grad, grad, grad, basis]
    if other is not None:
        in_specs.append(pl.BlockSpec(tile, lambda step, place: (other_at, 0, 0, 0, 0)))
        operands.append(other)
    count = len(shifts)
    return pl.pallas_call(
        functools.partial(project_kernel, other is not None),
        out_shape=jax.ShapeDtypeStruct((count, 4, 4, 128, 256), bf16),
        grid_spec=pltpu.PrefetchScalarGridSpec(
            num_scalar_prefetch=1,
            grid=(count,),
            in_specs=in_specs,
            out_specs=pl.BlockSpec(tile, lambda step, place: (step, 0, 0, 0, 0)),
        ),
        compiler_params=pltpu.CompilerParams(vmem_limit_bytes=24 << 20),
        cost_estimate=pl.CostEstimate(
            flops=count, bytes_accessed=count, transcendentals=0
        ),
    )(*operands)


def project_up_kernel(place_ref, basis_ref, *refs):
    grad_refs, before_ref, out_ref, sum_ref = refs[:8], refs[8:-2], refs[-2], refs[-1]
    step = pl.program_id(0)

    @pl.when(step == 0)
    def _():
        sum_ref[...] = before_ref[0][...] if before_ref else jnp.zeros_like(sum_ref)

    parts = [
        lax.dot_general(
            basis_ref[part // 4, part % 4],
            grad_ref[...],
            (((0,), (0,)), ((), ())),
            preferred_element_type=f32,
        )
        for part, grad_ref in enumerate(grad_refs)
    ]
    sum_ref[...] += functools.reduce(lambda a, b: a + b, parts)

    @pl.when(step == 1)
    def _():
        out_ref[...] = sum_ref[...].astype(out_ref.dtype)


def project_up(place, basis, grad, own, before=None):
    def grad_map(part):
        def index(step, place):
            x = (place[1] + 4 - part % 4) % 4
            y = (place[3] + 4 - part // 4 - 2 * step) % 4
            return ((x * 4 + y) * 2 + place_of(place, own), 0)

        return index

    whole = pl.BlockSpec((256, 512), lambda step, place: (0, 0))
    in_specs = [pl.BlockSpec((2, 4, 256, 256), lambda step, place: (step, 0, 0, 0))]
    in_specs += [pl.BlockSpec((256, 512), grad_map(part)) for part in range(8)]
    operands = [place, basis] + [grad] * 8
    if before is not None:
        in_specs.append(whole)
        operands.append(before)
    return pl.pallas_call(
        project_up_kernel,
        out_shape=jax.ShapeDtypeStruct((256, 512), f32 if before is None else bf16),
        grid_spec=pltpu.PrefetchScalarGridSpec(
            num_scalar_prefetch=1,
            grid=(2,),
            in_specs=in_specs,
            out_specs=whole,
            scratch_shapes=[pltpu.VMEM((256, 512), f32)],
        ),
        compiler_params=pltpu.CompilerParams(vmem_limit_bytes=60 << 20),
        cost_estimate=pl.CostEstimate(
            flops=1, bytes_accessed=1, transcendentals=0
        ),
    )(*operands)


def sum_kernel(place_ref, own_ref, *refs):
    got_refs, next_ref, out_refs = refs[:3], refs[3], refs[4:]
    start = jnp.where(place_ref[2] == 0, place_ref[1], place_ref[0])
    for ahead, out_ref in zip((0, 2, 1, 3), (next_ref, *out_refs), strict=True):
        at = (start + ahead) % 4
        value = own_ref[at].astype(f32)
        for got_ref in got_refs:
            value = value + got_ref[at].astype(f32)
        out_ref[...] = value.astype(out_ref.dtype)


def sum_blocks(place, own, got):
    vmem = pl.BlockSpec(memory_space=pltpu.VMEM)
    block = jax.ShapeDtypeStruct((4, 128, 256), bf16)
    return pl.pallas_call(
        sum_kernel,
        out_shape=[jax.ShapeDtypeStruct((4, 128, 256), f32), block, block, block],
        in_specs=[pl.BlockSpec(memory_space=pltpu.SMEM)] + [vmem] * 4,
        out_specs=[vmem] * 4,
        compiler_params=pltpu.CompilerParams(vmem_limit_bytes=24 << 20),
        cost_estimate=pl.CostEstimate(flops=4 << 20, bytes_accessed=5 << 20, transcendentals=0),
    )(place, own, *got)


def norms_kernel(weights_ref, *refs):
    low_refs, (basis_down_ref, other_down_ref) = refs[:4], refs[4:6]
    own_ref, other_ref, low_up_ref, out_ref = refs[6:]

    def square_sum(delta):
        return jnp.sum(jnp.sum(delta * delta, axis=0, keepdims=True), axis=1, keepdims=True)

    up = jnp.zeros((1, 1), f32)
    for ref in (own_ref, other_ref):
        for block in range(4):
            up += square_sum(jnp.dot(ref[block], low_up_ref[...], preferred_element_type=f32))
    down = jnp.zeros((1, 1), f32)
    for low_ref in low_refs:
        for ref in (basis_down_ref, other_down_ref):
            down += square_sum(
                lax.dot_general(
                    low_ref[...].reshape(512, 256),
                    ref[...],
                    (((1,), (1,)), ((), ())),
                    preferred_element_type=f32,
                )
            )
    lane = lax.broadcasted_iota(jnp.int32, (1, 128), 1)
    row = jnp.where(lane == 0, weights_ref[0], weights_ref[1])
    row = jnp.where(lane == 2, up, jnp.where(lane == 3, down, row))
    out_ref[...] = jnp.broadcast_to(row[None], out_ref.shape)


def norms(weight_sums, lows, basis_down, other_down, own, other, low_up):
    vmem = pl.BlockSpec(memory_space=pltpu.VMEM)
    operands = [weight_sums, *lows, basis_down, other_down, own, other, low_up]
    return pl.pallas_call(
        norms_kernel,
        out_shape=jax.ShapeDtypeStruct((128, 1, 128), f32),
        in_specs=[pl.BlockSpec(memory_space=pltpu.SMEM)] + [vmem] * (len(operands) - 1),
        out_specs=vmem,
        compiler_params=pltpu.CompilerParams(vmem_limit_bytes=16 << 20),
        cost_estimate=pl.CostEstimate(
            flops=1 << 34, bytes_accessed=3 << 20, transcendentals=0
        ),
    )(*operands)


def update_kernel(place_ref, sums_ref, *refs):
    low_refs, (basis_down_ref, weight_down_ref) = refs[:8], refs[8:10]
    own_ref, other_ref, low_up_hbm, weight_up_hbm, up_hbm, down_hbm = refs[10:16]
    low_up_ref, weight_up_ref, up_ref, down_ref, in_sems, out_sems = refs[16:]
    loads = [
        pltpu.make_async_copy(low_up_hbm, low_up_ref, in_sems.at[0]),
        pltpu.make_async_copy(weight_up_hbm, weight_up_ref, in_sems.at[1]),
    ]
    for copy in loads:
        copy.start()
    sums = jnp.sum(sums_ref[...], axis=0)
    scale_up = learn_rate * (jnp.sqrt(sums[:, 0:1]) / (jnp.sqrt(sums[:, 2:3]) + norm_eps))
    scale_down = learn_rate * (jnp.sqrt(sums[:, 1:2]) / (jnp.sqrt(sums[:, 3:4]) + norm_eps))
    core0 = place_ref[2]
    for i, low_ref in enumerate(low_refs):
        outer = i % 4
        core = core0 if i < 4 else 1 - core0
        delta = lax.dot_general(
            low_ref[...].reshape(512, 256),
            basis_down_ref[...],
            (((1,), (1,)), ((), ())),
            preferred_element_type=f32,
        )
        for inner in range(4):
            x = (place_ref[1] + 4 - jnp.where(core == 0, outer, inner)) % 4
            y = (place_ref[3] + 4 - jnp.where(core == 0, inner, outer)) % 4
            old = weight_down_ref[x, y, core].astype(f32)
            down_ref[x, y, core] = (
                old - scale_down * delta[inner * 128 : (inner + 1) * 128]
            ).astype(bf16)
    stores = [pltpu.make_async_copy(down_ref, down_hbm, out_sems.at[4])]
    stores[0].start()
    for copy in loads:
        copy.wait()
    for y in range(4):
        back = (place_ref[3] + 4 - y) % 4
        for basis_ref, core in ((own_ref, core0), (other_ref, 1 - core0)):
            delta = jnp.dot(basis_ref[back], low_up_ref[...], preferred_element_type=f32)
            old = weight_up_ref[y, core].astype(f32)
            up_ref[y, core] = (old - scale_up * delta).astype(bf16)
        stores.append(pltpu.make_async_copy(up_ref.at[y], up_hbm.at[y], out_sems.at[y]))
        stores[-1].start()
    for copy in stores:
        copy.wait()


def update(place, sums, lows, basis_down, weight_down, own, other, low_up, weight_up):
    vmem = pl.BlockSpec(memory_space=pltpu.VMEM)
    hbm = pl.BlockSpec(memory_space=pltpu.HBM)
    operands = [place, sums, *lows, basis_down, weight_down, own, other, low_up, weight_up]
    return pl.pallas_call(
        update_kernel,
        out_shape=[
            jax.ShapeDtypeStruct(weight_up.shape, bf16),
            jax.ShapeDtypeStruct(weight_down.shape, bf16),
        ],
        in_specs=[pl.BlockSpec(memory_space=pltpu.SMEM)] + [vmem] * (len(operands) - 3) + [hbm] * 2,
        out_specs=[hbm, hbm],
        scratch_shapes=[
            pltpu.VMEM(low_up.shape, bf16),
            pltpu.VMEM(weight_up.shape, bf16),
            pltpu.VMEM(weight_up.shape, bf16),
            pltpu.VMEM(weight_down.shape, bf16),
            pltpu.SemaphoreType.DMA((2,)),
            pltpu.SemaphoreType.DMA((5,)),
        ],
        compiler_params=pltpu.CompilerParams(vmem_limit_bytes=24 << 20),
        cost_estimate=pl.CostEstimate(
            flops=4 * 2048 * 256 * 512, bytes_accessed=11 << 20, transcendentals=0
        ),
    )(*operands)


def after(value, *others):
    return lax.optimization_barrier((value, *others))[0]


def total(stages, first):
    return functools.reduce(lambda a, b: a + b.astype(f32), stages, first.astype(f32))


def per_device(
    weight_up,
    weight_down,
    grad_up,
    grad_down,
    basis_up,
    basis_down,
    moment_up,
    second_up,
    moment_down,
    second_down,
):
    z, x, y, c = (lax.axis_index(a) for a in AXES)
    replicas = 4
    local_up = grad_up[0]
    local_down = grad_down[0].reshape(4, 4, 4, 2, 128, 256)

    place = jnp.stack([z, x, c, y]).astype(jnp.int32)

    near = jnp.stack([basis_up] + [shift(basis_up, "x", "x", k) for k in (1, 2, 3)])
    weight_upf = weight_up.astype(f32)
    weight_downf = weight_down.astype(f32)
    wsq_up = jnp.sum(weight_upf * weight_upf)
    wsq_down = jnp.sum(weight_downf * weight_downf)

    half = functools.partial(project_rows, place, local_down, basis_down, False)
    whole = functools.partial(project_rows, place, local_down, basis_down, True)
    half_2 = half((2,))
    got_2 = swap_cores(half_2)
    ready = {2: whole((2,), got_2)[0]}
    half_130 = project_rows(
        after(place, ready[2], near), local_down, basis_down, False, (1, 3, 0)
    )
    got_130 = swap_cores(half_130)
    ready[1] = whole((1,), got_130, 0)[0]
    ready[3] = whole((3,), after(got_130, ready[1]), 1)[0]
    ready[0] = whole((0,), after(got_130, ready[3]), 2)[0]
    one = [shift(ready[k], "z", "x", k) for k in (2, 1, 3)]

    two_own, *two = sum_blocks(after(place, wsq_up, wsq_down), ready[0], one)
    two = [two_own] + [shift(t, "x", "z", k) for t, k in zip(two, (2, 1, 3))]

    back, ahead = shift(near, "y", "y", 1), shift(near, "y", "y", 3)
    back_half, ahead_half = after(back[:2], ready[0]), after(ahead[2:], ready[0])
    far = jnp.concatenate([shift(back_half, "y", "y", 1), shift(ahead_half, "y", "y", 3)])
    own_basis = jnp.stack([after(near, two_own), back, far, ahead])
    other_basis = swap_cores(own_basis)

    other_basis_down = swap_cores(after(basis_down, two_own))
    partial_up = project_up(place, own_basis, local_up, True)
    two[0] = after(two[0], partial_up)
    partial_up = project_up(place, other_basis, local_up, False, partial_up)
    partial_up = partial_up.reshape(4, 64, 512)

    mine, theirs = (z, 3 - z), (z ^ 1, 3 - (z ^ 1))
    half_up = jnp.stack([pick(partial_up, block) for block in theirs])
    half_up = exchange(half_up, 1).astype(f32)
    half_up = half_up + jnp.stack([pick(partial_up, block) for block in mine]).astype(f32)

    def part_three(k):
        index = (y + k) % 4
        return total([pick(t, index) for t in two[1:]], pick(two[0], index))

    three = [part_three(0)] + [
        shift(part_three(k).astype(bf16), "y", "y", k) for k in (2, 1, 3)
    ]
    three[0] = after(three[0], partial_up)
    proj_down = total(three[1:], three[0]) * (1.0 / replicas)
    new_moment_down, new_second_down, low_down = adam_update(proj_down, moment_down, second_down)

    proj_up = (half_up[0] + exchange(half_up[1].astype(bf16), 3).astype(f32)) * (1.0 / replicas)
    new_moment_up, new_second_up, low_up = adam_update(proj_up, moment_up, second_up)
    pair_up = jnp.stack([low_up, exchange(low_up, 3)])
    all_up = jnp.concatenate([pair_up, exchange(pair_up, 1)])
    order = [
        jnp.where(block == z, 0, jnp.where(block == 3 - z, 1, jnp.where(block == z ^ 1, 2, 3)))
        for block in range(4)
    ]
    all_low_up = jnp.stack([pick(all_up, at) for at in order]).reshape(256, 512)

    blocks = [
        lax.dynamic_index_in_dim(basis, (x + 4 - z) % 4, 1, keepdims=False)
        for basis in (own_basis, other_basis)
    ]

    inner = jnp.stack([low_down] + [shift(low_down, "y", "x", k) for k in (1, 2, 3)])
    outer = [inner] + [shift(inner, "x", "y", k) for k in (1, 2, 3)]
    sibling = [swap_cores(low) for low in outer]

    sums = norms(
        jnp.stack([wsq_up, wsq_down]),
        outer,
        basis_down,
        other_basis_down,
        *blocks,
        all_low_up,
    )
    sums = after(sums, *sibling)
    sums = lax.all_to_all(sums, AXES, 0, 0, tiled=True)
    new_weight_up, new_weight_down = update(
        place,
        sums,
        outer + sibling,
        basis_down,
        weight_down.reshape(4, 4, 2, 128, 256),
        *blocks,
        all_low_up,
        weight_up.reshape(4, 2, 256, 512),
    )
    new_weight_up = new_weight_up.reshape(2048, 512)
    new_weight_down = new_weight_down.reshape(4096, 256)
    return (
        new_weight_up,
        new_weight_down,
        new_moment_up,
        new_second_up,
        new_moment_down,
        new_second_down,
    )


def solution(mesh):
    devices = Mesh(mesh.devices.reshape(SIZES), AXES)
    columns = ("x", "y", "c")
    in_specs = (
        P("z", columns),
        P("z", columns),
        P("z", None, columns),
        P("z", None, columns),
        P(columns, None),
        P(columns, None),
        P("z", columns),
        P("z", columns),
        P(AXES, None),
        P(AXES, None),
    )
    out_specs = (
        P("z", columns),
        P("z", columns),
        P("z", columns),
        P("z", columns),
        P(AXES, None),
        P(AXES, None),
    )
    return jax.shard_map(
        per_device, mesh=devices, in_specs=in_specs, out_specs=out_specs, check_vma=False
    )
```

```python
import functools

import jax
import jax.numpy as jnp
from jax import lax
from jax.experimental import pallas as pl
from jax.experimental.pallas import tpu as pltpu
from jax.sharding import Mesh, PartitionSpec as P

ADAM_STEP = 10

first_decay = 0.9
second_decay = 0.99
adam_eps = 1e-08
norm_eps = 1e-06
learn_rate = 0.5

f32 = jnp.float32
bf16 = jnp.bfloat16

AXES = ("z", "x", "y", "c")
SIZES = (4, 4, 4, 2)


def adam_update(mean_grad, first, second):
    new_first = first_decay * first + (1.0 - first_decay) * mean_grad
    new_second = second_decay * second + (1.0 - second_decay) * mean_grad * mean_grad
    corr_first = 1.0 - first_decay**ADAM_STEP
    corr_second = 1.0 - second_decay**ADAM_STEP
    update = (new_first / corr_first / (jnp.sqrt(new_second / corr_second) + adam_eps)).astype(
        bf16
    )
    return (new_first, new_second, update)


def shift_pairs(axis0, axis1, k):
    pairs = []
    for source in range(128):
        coords = [source // 32, source // 8 % 4, source // 2 % 4, source % 2]
        dim = AXES.index(axis1 if coords[3] else axis0)
        coords[dim] = (coords[dim] + k) % 4
        target = ((coords[0] * 4 + coords[1]) * 4 + coords[2]) * 2 + coords[3]
        pairs.append((source, target))
    return pairs


def shift(value, axis0, axis1, k):
    return lax.ppermute(value, AXES, shift_pairs(axis0, axis1, k))


def swap_cores(value):
    return lax.ppermute(value, "c", [(0, 1), (1, 0)])


def exchange(value, mask):
    return lax.ppermute(value, "z", [(i, i ^ mask) for i in range(4)])


def pick(stacked, index):
    return lax.dynamic_index_in_dim(stacked, index, 0, keepdims=False)


def place_of(place, own):
    return place[2] if own else 1 - place[2]


def project_kernel(has_other, place_ref, *refs):
    grad_refs, basis_ref, out_ref = refs[:4], refs[4], refs[-1]
    for part, grad_ref in enumerate(grad_refs):
        rows = grad_ref[...].reshape(512, 256)
        out = jnp.dot(rows, basis_ref[...], preferred_element_type=f32)
        if has_other:
            out = out + refs[5][0, part].reshape(512, 256).astype(f32)
        out_ref[0, part] = out.astype(bf16).reshape(4, 128, 256)


def project_rows(place, grad, basis, own, shifts, other=None, other_at=0):
    def grad_map(part):
        def index(step, place):
            core = place_of(place, own)
            ahead = shifts[-1]
            for i, shift_by in enumerate(shifts[:-1]):
                ahead = jnp.where(step == i, shift_by, ahead)
            block = (jnp.where(core == 0, place[0], place[1]) + ahead) % 4
            return (
                jnp.where(core == 0, block, part),
                jnp.where(core == 0, part, block),
                0,
                core,
                0,
                0,
            )

        return index

    tile = (1, 4, 4, 128, 256)
    in_specs = [pl.BlockSpec((1, 1, 4, 1, 128, 256), grad_map(part)) for part in range(4)]
    in_specs.append(pl.BlockSpec((256, 256), lambda step, place: (0, 0)))
    operands = [place, grad, grad, grad, grad, basis]
    if other is not None:
        in_specs.append(pl.BlockSpec(tile, lambda step, place: (other_at, 0, 0, 0, 0)))
        operands.append(other)
    count = len(shifts)
    return pl.pallas_call(
        functools.partial(project_kernel, other is not None),
        out_shape=jax.ShapeDtypeStruct((count, 4, 4, 128, 256), bf16),
        grid_spec=pltpu.PrefetchScalarGridSpec(
            num_scalar_prefetch=1,
            grid=(count,),
            in_specs=in_specs,
            out_specs=pl.BlockSpec(tile, lambda step, place: (step, 0, 0, 0, 0)),
        ),
        compiler_params=pltpu.CompilerParams(vmem_limit_bytes=24 << 20),
        cost_estimate=pl.CostEstimate(
            flops=count, bytes_accessed=count, transcendentals=0
        ),
    )(*operands)


def project_up_kernel(place_ref, basis_ref, *refs):
    grad_refs, sum_ref = refs[:8], refs[-1]
    before_ref, out_refs = (refs[8:9], refs[9:11]) if len(refs) > 10 else ((), refs[8:9])
    step = pl.program_id(0)

    @pl.when(step == 0)
    def _():
        sum_ref[...] = before_ref[0][...] if before_ref else jnp.zeros_like(sum_ref)

    parts = [
        lax.dot_general(
            basis_ref[part // 4, part % 4],
            grad_ref[...],
            (((0,), (0,)), ((), ())),
            preferred_element_type=f32,
        )
        for part, grad_ref in enumerate(grad_refs)
    ]
    sum_ref[...] += functools.reduce(lambda a, b: a + b, parts)

    @pl.when(step == 1)
    def _():
        if not before_ref:
            out_refs[0][...] = sum_ref[...]
            return
        z = place_ref[0]
        for out_ref, first in zip(out_refs, (z ^ 1, z), strict=True):
            for i, block in enumerate((first, 3 - first)):
                rows = pl.ds(pl.multiple_of(block * 64, 64), 64)
                out_ref[i] = sum_ref[rows, :].astype(out_ref.dtype)


def project_up(place, basis, grad, own, before=None):
    def grad_map(part):
        def index(step, place):
            x = (place[1] + 4 - part % 4) % 4
            y = (place[3] + 4 - part // 4 - 2 * step) % 4
            return ((x * 4 + y) * 2 + place_of(place, own), 0)

        return index

    whole = pl.BlockSpec((256, 512), lambda step, place: (0, 0))
    in_specs = [pl.BlockSpec((2, 4, 256, 256), lambda step, place: (step, 0, 0, 0))]
    in_specs += [pl.BlockSpec((256, 512), grad_map(part)) for part in range(8)]
    operands = [place, basis] + [grad] * 8
    if before is not None:
        in_specs.append(whole)
        operands.append(before)
    if before is None:
        out_shape, out_specs = jax.ShapeDtypeStruct((256, 512), f32), whole
    else:
        pair = pl.BlockSpec((2, 64, 512), lambda step, place: (0, 0, 0))
        out_shape = [jax.ShapeDtypeStruct((2, 64, 512), t) for t in (bf16, f32)]
        out_specs = [pair, pair]
    return pl.pallas_call(
        project_up_kernel,
        out_shape=out_shape,
        grid_spec=pltpu.PrefetchScalarGridSpec(
            num_scalar_prefetch=1,
            grid=(2,),
            in_specs=in_specs,
            out_specs=out_specs,
            scratch_shapes=[pltpu.VMEM((256, 512), f32)],
        ),
        compiler_params=pltpu.CompilerParams(vmem_limit_bytes=60 << 20),
        cost_estimate=pl.CostEstimate(
            flops=1, bytes_accessed=1, transcendentals=0
        ),
    )(*operands)


def sum_kernel(place_ref, own_ref, *refs):
    got_refs, next_ref, out_refs = refs[:3], refs[3], refs[4:]
    start = jnp.where(place_ref[2] == 0, place_ref[1], place_ref[0])
    for ahead, out_ref in zip((0, 2, 1, 3), (next_ref, *out_refs), strict=True):
        at = (start + ahead) % 4
        value = own_ref[at].astype(f32)
        for got_ref in got_refs:
            value = value + got_ref[at].astype(f32)
        out_ref[...] = value.astype(out_ref.dtype)


def sum_blocks(place, own, got):
    vmem = pl.BlockSpec(memory_space=pltpu.VMEM)
    block = jax.ShapeDtypeStruct((4, 128, 256), bf16)
    return pl.pallas_call(
        sum_kernel,
        out_shape=[jax.ShapeDtypeStruct((4, 128, 256), f32), block, block, block],
        in_specs=[pl.BlockSpec(memory_space=pltpu.SMEM)] + [vmem] * 4,
        out_specs=[vmem] * 4,
        compiler_params=pltpu.CompilerParams(vmem_limit_bytes=24 << 20),
        cost_estimate=pl.CostEstimate(flops=4 << 20, bytes_accessed=5 << 20, transcendentals=0),
    )(place, own, *got)


def basis_copies(place_ref, hbm_refs, refs, sems):
    column = (place_ref[1] + 4 - place_ref[0]) % 4
    return [
        pltpu.make_async_copy(hbm_ref.at[:, column], ref, sems.at[i])
        for i, (hbm_ref, ref) in enumerate(zip(hbm_refs, refs, strict=True))
    ]


def norms_kernel(place_ref, up_weight_ref, down_weight_ref, *refs):
    low_refs, (basis_down_ref, other_down_ref) = refs[:4], refs[4:6]
    own_hbm, other_hbm, low_up_ref, out_ref, own_ref, other_ref, sems = refs[6:]
    copies = basis_copies(place_ref, (own_hbm, other_hbm), (own_ref, other_ref), sems)
    for copy in copies:
        copy.start()

    def square_sum(delta):
        return jnp.sum(jnp.sum(delta * delta, axis=0, keepdims=True), axis=1, keepdims=True)

    down = jnp.zeros((1, 1), f32)
    for low_ref in low_refs:
        for ref in (basis_down_ref, other_down_ref):
            down += square_sum(
                lax.dot_general(
                    low_ref[...].reshape(512, 256),
                    ref[...],
                    (((1,), (1,)), ((), ())),
                    preferred_element_type=f32,
                )
            )
    for copy in copies:
        copy.wait()
    up = jnp.zeros((1, 1), f32)
    for ref in (own_ref, other_ref):
        for block in range(4):
            up += square_sum(jnp.dot(ref[block], low_up_ref[...], preferred_element_type=f32))
    lane = lax.broadcasted_iota(jnp.int32, (1, 128), 1)
    row = jnp.where(lane == 0, up_weight_ref[0], down_weight_ref[0])
    row = jnp.where(lane == 2, up, jnp.where(lane == 3, down, row))
    out_ref[...] = jnp.broadcast_to(row[None], out_ref.shape)


def norms(place, up_weight, down_weight, lows, basis_down, other_down, own, other, low_up):
    vmem = pl.BlockSpec(memory_space=pltpu.VMEM)
    smem = pl.BlockSpec(memory_space=pltpu.SMEM)
    hbm = pl.BlockSpec(memory_space=pltpu.HBM)
    operands = [place, up_weight, down_weight, *lows, basis_down, other_down, own, other, low_up]
    return pl.pallas_call(
        norms_kernel,
        out_shape=jax.ShapeDtypeStruct((128, 1, 128), f32),
        in_specs=[smem] * 3 + [vmem] * 6 + [hbm] * 2 + [vmem],
        out_specs=vmem,
        scratch_shapes=[
            pltpu.VMEM((4, 256, 256), bf16),
            pltpu.VMEM((4, 256, 256), bf16),
            pltpu.SemaphoreType.DMA((2,)),
        ],
        compiler_params=pltpu.CompilerParams(vmem_limit_bytes=16 << 20),
        cost_estimate=pl.CostEstimate(
            flops=1 << 34, bytes_accessed=3 << 20, transcendentals=0
        ),
    )(*operands)


def update_kernel(place_ref, sums_ref, *refs):
    low_refs, (basis_down_ref, weight_down_ref) = refs[:8], refs[8:10]
    own_hbm, other_hbm, low_up_hbm, weight_up_hbm, up_hbm, down_hbm = refs[10:16]
    own_ref, other_ref, low_up_ref, weight_up_ref, up_ref, down_ref = refs[16:22]
    in_sems, basis_sems, out_sems = refs[22:]
    loads = basis_copies(place_ref, (own_hbm, other_hbm), (own_ref, other_ref), basis_sems)
    loads += [
        pltpu.make_async_copy(low_up_hbm, low_up_ref, in_sems.at[0]),
        pltpu.make_async_copy(weight_up_hbm, weight_up_ref, in_sems.at[1]),
    ]
    for copy in loads:
        copy.start()
    sums = jnp.sum(sums_ref[...], axis=0)
    scale_up = learn_rate * (jnp.sqrt(sums[:, 0:1]) / (jnp.sqrt(sums[:, 2:3]) + norm_eps))
    scale_down = learn_rate * (jnp.sqrt(sums[:, 1:2]) / (jnp.sqrt(sums[:, 3:4]) + norm_eps))
    core0 = place_ref[2]
    for i, low_ref in enumerate(low_refs):
        outer = i % 4
        core = core0 if i < 4 else 1 - core0
        delta = lax.dot_general(
            low_ref[...].reshape(512, 256),
            basis_down_ref[...],
            (((1,), (1,)), ((), ())),
            preferred_element_type=f32,
        )
        for inner in range(4):
            x = (place_ref[1] + 4 - jnp.where(core == 0, outer, inner)) % 4
            y = (place_ref[3] + 4 - jnp.where(core == 0, inner, outer)) % 4
            old = weight_down_ref[x, y, core].astype(f32)
            down_ref[x, y, core] = (
                old - scale_down * delta[inner * 128 : (inner + 1) * 128]
            ).astype(bf16)
    stores = [pltpu.make_async_copy(down_ref, down_hbm, out_sems.at[4])]
    stores[0].start()
    for copy in loads:
        copy.wait()
    for y in range(4):
        back = (place_ref[3] + 4 - y) % 4
        for basis_ref, core in ((own_ref, core0), (other_ref, 1 - core0)):
            delta = jnp.dot(basis_ref[back], low_up_ref[...], preferred_element_type=f32)
            old = weight_up_ref[y, core].astype(f32)
            up_ref[y, core] = (old - scale_up * delta).astype(bf16)
        stores.append(pltpu.make_async_copy(up_ref.at[y], up_hbm.at[y], out_sems.at[y]))
        stores[-1].start()
    for copy in stores:
        copy.wait()


def update(place, sums, lows, basis_down, weight_down, own, other, low_up, weight_up):
    vmem = pl.BlockSpec(memory_space=pltpu.VMEM)
    hbm = pl.BlockSpec(memory_space=pltpu.HBM)
    operands = [place, sums, *lows, basis_down, weight_down, own, other, low_up, weight_up]
    return pl.pallas_call(
        update_kernel,
        out_shape=[
            jax.ShapeDtypeStruct(weight_up.shape, bf16),
            jax.ShapeDtypeStruct(weight_down.shape, bf16),
        ],
        in_specs=[pl.BlockSpec(memory_space=pltpu.SMEM)] + [vmem] * (len(operands) - 5) + [hbm] * 4,
        out_specs=[hbm, hbm],
        scratch_shapes=[
            pltpu.VMEM((4, 256, 256), bf16),
            pltpu.VMEM((4, 256, 256), bf16),
            pltpu.VMEM(low_up.shape, bf16),
            pltpu.VMEM(weight_up.shape, bf16),
            pltpu.VMEM(weight_up.shape, bf16),
            pltpu.VMEM(weight_down.shape, bf16),
            pltpu.SemaphoreType.DMA((2,)),
            pltpu.SemaphoreType.DMA((2,)),
            pltpu.SemaphoreType.DMA((5,)),
        ],
        compiler_params=pltpu.CompilerParams(vmem_limit_bytes=24 << 20),
        cost_estimate=pl.CostEstimate(
            flops=4 * 2048 * 256 * 512, bytes_accessed=11 << 20, transcendentals=0
        ),
    )(*operands)


def after(value, *others):
    return lax.optimization_barrier((value, *others))[0]


def total(stages, first):
    return functools.reduce(lambda a, b: a + b.astype(f32), stages, first.astype(f32))


def per_device(
    weight_up,
    weight_down,
    grad_up,
    grad_down,
    basis_up,
    basis_down,
    moment_up,
    second_up,
    moment_down,
    second_down,
):
    z, x, y, c = (lax.axis_index(a) for a in AXES)
    replicas = 4
    local_up = grad_up[0]
    local_down = grad_down[0].reshape(4, 4, 4, 2, 128, 256)

    place = jnp.stack([z, x, c, y]).astype(jnp.int32)

    near = jnp.stack([basis_up] + [shift(basis_up, "x", "x", k) for k in (1, 2, 3)])
    weight_upf = weight_up.astype(f32)
    weight_downf = weight_down.astype(f32)
    wsq_up = jnp.sum(weight_upf * weight_upf)
    wsq_down = jnp.sum(weight_downf * weight_downf)

    half = functools.partial(project_rows, place, local_down, basis_down, False)
    whole = functools.partial(project_rows, place, local_down, basis_down, True)
    half_2 = half((2,))
    got_2 = swap_cores(half_2)
    ready = {2: whole((2,), got_2)[0]}
    half_130 = project_rows(
        after(place, ready[2], near), local_down, basis_down, False, (1, 3, 0)
    )
    got_130 = swap_cores(half_130)
    ready[1] = whole((1,), got_130, 0)[0]
    ready[3] = whole((3,), after(got_130, ready[1]), 1)[0]
    ready[0] = whole((0,), after(got_130, ready[3]), 2)[0]
    one = [shift(ready[k], "z", "x", k) for k in (2, 1, 3)]

    two_own, *two = sum_blocks(after(place, wsq_up, wsq_down), ready[0], one)
    two = [two_own] + [shift(t, "x", "z", k) for t, k in zip(two, (2, 1, 3))]

    back, ahead = shift(near, "y", "y", 1), shift(near, "y", "y", 3)
    back_half, ahead_half = after(back[:2], ready[0]), after(ahead[2:], ready[0])
    far = jnp.concatenate([shift(back_half, "y", "y", 1), shift(ahead_half, "y", "y", 3)])
    own_basis = jnp.stack([after(near, two_own), back, far, ahead])
    other_basis = swap_cores(own_basis)

    other_basis_down = swap_cores(after(basis_down, two_own))
    partial_up = project_up(place, own_basis, local_up, True)
    two[0] = after(two[0], partial_up)

    theirs, mine = project_up(place, other_basis, local_up, False, partial_up)
    half_up = exchange(theirs, 1).astype(f32) + mine

    def part_three(k):
        index = (y + k) % 4
        return total([pick(t, index) for t in two[1:]], pick(two[0], index))

    three = [part_three(0)] + [
        shift(part_three(k).astype(bf16), "y", "y", k) for k in (2, 1, 3)
    ]
    three[0] = after(three[0], mine)
    proj_down = total(three[1:], three[0]) * (1.0 / replicas)
    new_moment_down, new_second_down, low_down = adam_update(proj_down, moment_down, second_down)

    proj_up = (half_up[0] + exchange(half_up[1].astype(bf16), 3).astype(f32)) * (1.0 / replicas)
    new_moment_up, new_second_up, low_up = adam_update(proj_up, moment_up, second_up)
    pair_up = jnp.stack([low_up, exchange(low_up, 3)])
    all_up = jnp.concatenate([pair_up, exchange(pair_up, 1)])
    order = [
        jnp.where(block == z, 0, jnp.where(block == 3 - z, 1, jnp.where(block == z ^ 1, 2, 3)))
        for block in range(4)
    ]
    all_low_up = jnp.stack([pick(all_up, at) for at in order]).reshape(256, 512)

    inner = jnp.stack([low_down] + [shift(low_down, "y", "x", k) for k in (1, 2, 3)])
    outer = [inner] + [shift(inner, "x", "y", k) for k in (1, 2, 3)]
    sibling = [swap_cores(low) for low in outer]

    sums = norms(
        place,
        wsq_up.reshape(1),
        wsq_down.reshape(1),
        outer,
        basis_down,
        other_basis_down,
        own_basis,
        other_basis,
        all_low_up,
    )
    sums = after(sums, *sibling)
    sums = lax.all_to_all(sums, AXES, 0, 0, tiled=True)
    new_weight_up, new_weight_down = update(
        place,
        sums,
        outer + sibling,
        basis_down,
        weight_down.reshape(4, 4, 2, 128, 256),
        own_basis,
        other_basis,
        all_low_up,
        weight_up.reshape(4, 2, 256, 512),
    )
    new_weight_up = new_weight_up.reshape(2048, 512)
    new_weight_down = new_weight_down.reshape(4096, 256)
    return (
        new_weight_up,
        new_weight_down,
        new_moment_up,
        new_second_up,
        new_moment_down,
        new_second_down,
    )


def solution(mesh):
    devices = Mesh(mesh.devices.reshape(SIZES), AXES)
    columns = ("x", "y", "c")
    in_specs = (
        P("z", columns),
        P("z", columns),
        P("z", None, columns),
        P("z", None, columns),
        P(columns, None),
        P(columns, None),
        P("z", columns),
        P("z", columns),
        P(AXES, None),
        P(AXES, None),
    )
    out_specs = (
        P("z", columns),
        P("z", columns),
        P("z", columns),
        P("z", columns),
        P(AXES, None),
        P(AXES, None),
    )
    return jax.shard_map(
        per_device, mesh=devices, in_specs=in_specs, out_specs=out_specs, check_vma=False
    )
```
